32 devices in a mesh: row: 4 (over y, x), col: 8 (over z, core).
Axes of the slice: x: 2, y: 2, z: 4, core: 2. Of those that a mesh axis runs over, the one named last changes fastest.
Arguments:
- coords: float32 [3, 4096], replicated, may hold values from 0 to 1
- lengths: float32 [3], replicated, may hold values from 0.4 to 1.2
- pattern: int32 [8, 8], replicated, may hold values from 0 to 1, as said below
- blocks: int32 [8], replicated, may hold values from 0 to 7, each once
- inverses: float32 [2, 512, 512], replicated, as said below
- earlier: bfloat16 [4096, 1024], P('row'), may hold values from -0.29882812 to 0.29882812
Outputs:
- schur: float32 [4096, 4096], P('row', 'col')
The draws below stay inside these ranges and needn't reach their ends.
Inputs may be any that keep to these rules, and one draw needn't show every extreme that they name: `pattern`: symmetric, with ones on the diagonal. `blocks`: each tile gets its own site block. `inverses`: each of the two factors is lower triangular with a positive diagonal.
All inputs are finite; a program needn't handle non-finite values.
Results may differ from the reference program's by a relative error of at most 0.0007.
Values may be sent and summed in bfloat16 or wider, within the bound.
A program may use at most 64 MiB of HBM per device.

```python
import math
import jax
import jax.numpy as jnp
from jax import lax

TB = 512
W = 1024
NT = 8
NSITE = 4096
N_ROW = 4
N_COL = 8


def draw_pattern(key, part):
    random_bits = jax.random.randint(jax.random.fold_in(key, 11), (NT, NT), 0, 2, dtype=jnp.int32)
    upper = jnp.triu(random_bits, 1)
    return (upper + upper.T + jnp.eye(NT, dtype=jnp.int32)).astype(jnp.int32)


def draw_inverses(key, part):
    off_key = jax.random.fold_in(key, 21)
    diag_key = jax.random.fold_in(key, 22)
    lower = jax.random.normal(off_key, (2, TB, TB), jnp.float32) * (0.1 / TB ** 0.5)
    diagonal = jax.random.uniform(diag_key, (2, TB), jnp.float32, 0.05, 0.15)
    eye_matrix = jnp.eye(TB, dtype=jnp.float32)
    return jnp.tril(lower, -1) + eye_matrix[None] * diagonal[:, None, :]


def steps_of(own_key, extent, shards, smallest, high):
    def one(dim, parts):
        draws = jax.random.uniform(jax.random.fold_in(jax.random.fold_in(own_key, 6), dim), (parts,), jnp.float32, smallest / len(shards), high / len(shards))
        return jnp.repeat(jnp.exp(draws), extent[dim] // parts).reshape((-1,) + (1,) * (len(extent) - dim - 1))

    factor_of = one(*shards[0])
    for cut in shards[1:]:
        factor_of = factor_of * one(*cut)
    return factor_of


def scatter_about(rng, dims, width, most, shards=(), kind=jnp.bfloat16):
    entries = width * jax.random.normal(rng, dims, jnp.float32)
    if shards:
        entries = entries * steps_of(rng, dims, shards, -0.22, 0.18)
    return jnp.clip(entries, -most, most).astype(kind)


def setup_inputs(seed: int = 0) -> dict:
    splits = jax.random.split(jax.random.key(seed), 7)
    coords = jnp.clip(jax.random.uniform(splits[0], (3, NSITE), jnp.float32, 0.0, 1.0), 0.0, 1.0)
    lengths = jnp.clip(jnp.exp(jax.random.uniform(splits[1], (3,), jnp.float32, math.log(0.4), math.log(1.2))), 0.4, 1.2)
    pattern = draw_pattern(jax.random.fold_in(splits[6], 71), 0)
    blocks = jax.random.permutation(splits[3], NT).astype(jnp.int32)
    inverses = draw_inverses(jax.random.fold_in(splits[6], 71), 0)
    earlier = scatter_about(splits[5], (NSITE, W), 0.05, 0.29882812, ((0, 4),))
    return {"coords": coords, "lengths": lengths, "pattern": pattern, "blocks": blocks, "inverses": inverses, "earlier": earlier}


def wendland(left_sites, right_sites):
    sq_dist = jnp.zeros((left_sites.shape[1], right_sites.shape[1]), jnp.float32)
    for component in range(3):
        offset = left_sites[component][:, None] - right_sites[component][None, :]
        sq_dist = sq_dist + offset * offset
    radius = jnp.sqrt(sq_dist)
    falloff = jnp.maximum(1.0 - radius, 0.0)
    return falloff ** 4 * (4.0 * radius + 1.0)

def outer_low(left_rows, right_rows):
    return lax.dot_general(left_rows, right_rows, (((1,), (1,)), ((), ())), preferred_element_type=jnp.float32)

def outer_high(left_rows, right_rows):
    return lax.dot_general(left_rows, right_rows, (((1,), (1,)), ((), ())), precision=lax.Precision.HIGHEST, preferred_element_type=jnp.float32)

def reference(coords, lengths, pattern, blocks, inverses, earlier):
    row_tiles_n = NT // N_ROW
    col_tiles_n = NT // N_COL
    positions = jnp.arange(NT, dtype=jnp.int32)
    row_order = positions % row_tiles_n * N_ROW + positions // row_tiles_n
    col_order = positions % col_tiles_n * N_COL + positions // col_tiles_n
    grouped = jnp.take(coords.reshape(3, NT, TB), blocks, axis=1) / lengths[:, None, None]
    row_sites = jnp.take(grouped, row_order, axis=1).reshape(3, NSITE)
    col_sites = jnp.take(grouped, col_order, axis=1).reshape(3, NSITE)
    patf = pattern.astype(jnp.float32)
    row_pattern = jnp.take(patf, row_order, axis=0)
    earlier_blocks = earlier.reshape(NT, TB, W)
    first_earlier = earlier_blocks[0]
    second_earlier = earlier_blocks[row_tiles_n]
    mask_first = jnp.repeat(row_pattern[:, 0], TB)
    mask_second = jnp.repeat(row_pattern[:, 1], TB)
    cov_first = wendland(row_sites, grouped[:, 0]) * mask_first[:, None]
    cov_first = cov_first - outer_low(earlier, first_earlier)
    first_panel = outer_high(cov_first, inverses[0])
    first_tile = first_panel[row_tiles_n * TB:row_tiles_n * TB + TB]
    cov_second = wendland(row_sites, grouped[:, 1]) * mask_second[:, None]
    cov_second = cov_second - outer_low(earlier, second_earlier) - outer_high(first_panel, first_tile)
    second_panel = outer_high(cov_second, inverses[1])
    col_pos = col_order % N_ROW * row_tiles_n + col_order // N_ROW
    col_earlier = jnp.take(earlier_blocks, col_pos, axis=0).reshape(NSITE, W)
    col_first = jnp.take(first_panel.reshape(NT, TB, TB), col_pos, axis=0).reshape(NSITE, TB)
    col_second = jnp.take(second_panel.reshape(NT, TB, TB), col_pos, axis=0).reshape(NSITE, TB)
    col_pattern = jnp.take(row_pattern, col_order, axis=1)

    def one_block(position):
        sites = lax.dynamic_slice_in_dim(row_sites, position * TB, TB, 1)
        mask_row = lax.dynamic_slice_in_dim(col_pattern, position, 1, 0)[0]
        cov = wendland(sites, col_sites).reshape(TB, NT, TB) * mask_row[None, :, None]
        cov = cov.reshape(TB, NSITE)
        rows_earlier = lax.dynamic_slice_in_dim(earlier, position * TB, TB, 0)
        rows_first = lax.dynamic_slice_in_dim(first_panel, position * TB, TB, 0)
        rows_second = lax.dynamic_slice_in_dim(second_panel, position * TB, TB, 0)
        return cov - outer_low(rows_earlier, col_earlier) - outer_high(rows_first, col_first) - outer_high(rows_second, col_second)
    schur = lax.map(one_block, positions)
    return schur.reshape(NSITE, NSITE)
```

```python
import functools

import jax
import jax.numpy as jnp
from jax import lax
from jax.experimental import pallas as pl
from jax.experimental.pallas import tpu as pltpu
from jax.sharding import PartitionSpec as P

MESH = pl.DeviceIdType.MESH
BF = jnp.bfloat16
F32 = jnp.float32
PANELS = 2
PANEL_CHUNKS = 4
COL_CHUNKS = 4
STRIP = 32


def nt_dot(left, right):
    return lax.dot_general(left, right, (((1,), (1,)), ((), ())), preferred_element_type=F32)


def split3(x, order):
    hi = x.astype(BF)
    lo = (x - hi.astype(F32)).astype(BF)
    return jnp.concatenate([hi, hi, lo] if order == 0 else [hi, lo, hi], axis=1)


def tile_list(n_row, row_tiles_n):
    r = lax.axis_index("row")
    c = lax.axis_index("col")
    own = [jnp.int32(t * n_row) + r for t in range(row_tiles_n)]
    return own + [c, jnp.int32(1), jnp.int32(0)]


def pick_sites(n_row, row_tiles_n, lengths, blocks, coords, sites):
    tb = sites.shape[2]
    for t, tile in enumerate(tile_list(n_row, row_tiles_n)):
        start = pl.multiple_of(blocks[tile] * tb, 128)
        for comp in range(3):
            sites[t, comp : comp + 1, :] = coords[comp : comp + 1, pl.ds(start, tb)] / lengths[comp]
        sites[t, 3:8, :] = jnp.zeros((5, tb), F32)


def kernel(
    n_row,
    n_col,
    pattern,
    sites,
    earlier,
    inverses,
    out,
    got,
    sites_t,
    cov,
    inv_f,
    inv_s,
    low0,
    low1,
    send_sem,
    recv_sem,
    pair_sem,
    copy_sem,
    inv_sem,
):
    tb = inverses.shape[1]
    row_tiles_n = earlier.shape[0] // tb
    r = lax.axis_index("row")
    c = lax.axis_index("col")
    half = lax.rem(c, 2)
    mate = c + 1 - 2 * half
    bits = []
    b = n_row // 2
    while b:
        bits.append(b)
        b //= 2

    def flip(b):
        on = lax.rem(lax.div(r, b), 2)
        return r + b - 2 * b * on

    def distance(root):
        total = 0
        for b in bits:
            a1 = lax.rem(lax.div(r, b), 2)
            a2 = lax.rem(lax.div(root, b), 2)
            total = total + b * lax.rem(a1 + a2, 2)
        return total

    col_root = lax.rem(c, n_row)
    col_slot = lax.div(c, n_row)
    roots = [jnp.int32(p) for p in range(PANELS)] + [col_root]
    slots = [jnp.int32(0)] * PANELS + [col_slot]
    dist = [distance(root) for root in roots]

    half_rows = tb // 2
    p_rows = half_rows // PANEL_CHUNKS
    c_rows = tb // COL_CHUNKS
    streams = []
    for k in range(PANEL_CHUNKS):
        for p in range(PANELS):
            streams.append((p, half * half_rows + k * p_rows, p_rows, True))
    for k in range(COL_CHUNKS):
        streams.append((PANELS, jnp.int32(k * c_rows), c_rows, False))

    def piece(s, from_own):
        buf, first, rows, _ = streams[s]
        if from_own:
            start = pl.multiple_of(slots[buf] * tb + first, 16)
            return earlier.at[pl.ds(start, rows)]
        return got.at[buf, pl.ds(pl.multiple_of(first, 16), rows)]

    def row_copy(s, n, from_own):
        return pltpu.make_async_remote_copy(
            src_ref=piece(s, from_own),
            dst_ref=piece(s, False),
            send_sem=send_sem.at[s, n],
            recv_sem=recv_sem.at[s],
            device_id=(flip(bits[n]), c),
            device_id_type=MESH,
        )

    def pair_copy(s):
        return pltpu.make_async_remote_copy(
            src_ref=piece(s, False),
            dst_ref=piece(s, False),
            send_sem=send_sem.at[s, len(bits)],
            recv_sem=pair_sem.at[s],
            device_id=(r, mate),
            device_id_type=MESH,
        )

    def pair_arrival(s):
        buf, _, rows, _ = streams[s]
        k = s // PANELS
        first = pl.multiple_of((1 - half) * half_rows + k * p_rows, 16)
        there = got.at[buf, pl.ds(first, rows)]
        return pltpu.make_async_remote_copy(
            src_ref=there,
            dst_ref=there,
            send_sem=send_sem.at[s, len(bits)],
            recv_sem=pair_sem.at[s],
            device_id=(r, mate),
            device_id_type=MESH,
        )

    def sends(s, n):
        return lax.rem(dist[streams[s][0]], 2 * bits[n]) == 0

    def own_copy(buf):
        start = pl.multiple_of(slots[buf] * tb, 16)
        return pltpu.make_async_copy(
            earlier.at[pl.ds(start, tb)], got.at[buf], copy_sem.at[buf]
        )

    inv_copy = pltpu.make_async_copy(inverses, inv_f, inv_sem)
    inv_copy.start()

    barrier = pltpu.get_barrier_semaphore()
    for b in bits:
        pl.semaphore_signal(barrier, inc=1, device_id=(flip(b), c), device_id_type=MESH)
    pl.semaphore_signal(barrier, inc=1, device_id=(r, mate), device_id_type=MESH)
    pl.semaphore_wait(barrier, len(bits) + 1)

    for s in range(len(streams)):
        @pl.when(dist[streams[s][0]] == 0)
        def _(s=s):
            for n in range(len(bits)):
                row_copy(s, n, True).start()

    for buf in range(PANELS + 1):
        @pl.when(dist[buf] == 0)
        def _(buf=buf):
            own_copy(buf).start()

    def relay(s):
        @pl.when(dist[streams[s][0]] != 0)
        def _():
            row_copy(s, 0, False).wait_recv()
            for n in range(len(bits)):
                @pl.when(sends(s, n))
                def _(n=n):
                    row_copy(s, n, False).start()
            if streams[s][3]:
                pair_copy(s).start()

    def arrived(buf):
        @pl.when(dist[buf] == 0)
        def _():
            own_copy(buf).wait()

        for s in range(len(streams)):
            if streams[s][0] == buf and streams[s][3]:
                @pl.when(dist[buf] != 0)
                def _(s=s):
                    pair_arrival(s).wait_recv()

    tiles = tile_list(n_row, row_tiles_n)
    n_left = row_tiles_n + 2
    at_col, at_one, at_zero = row_tiles_n, row_tiles_n + 1, row_tiles_n + 2
    for t in range(n_left):
        sites_t[t] = sites[t].T

    def wendland(slot, left, right):
        keep = pattern[tiles[left], tiles[right]].astype(F32)

        def strip(i, carry):
            rows = pl.ds(pl.multiple_of(i * STRIP, STRIP), STRIP)
            at = sites_t[left, rows, :]
            sq = None
            for comp in range(3):
                off = at[:, comp : comp + 1] - sites[right, comp : comp + 1, :]
                sq = off * off if sq is None else sq + off * off
            radius = jnp.sqrt(sq)
            fall = jnp.maximum(1.0 - radius, 0.0)
            fall = fall * fall
            cov[slot, rows, :] = fall * fall * (4.0 * radius + 1.0) * keep
            return carry

        lax.fori_loop(0, tb // STRIP, strip, 0)

    def slot0(t):
        return t

    def slot1(t):
        return n_left + t

    def slot_out(t):
        return n_left + row_tiles_n + 1 + t

    covs = [(slot0(t), t, at_zero) for t in range(n_left)]
    covs += [(slot1(t), t, at_one) for t in range(row_tiles_n + 1)]
    covs += [(slot_out(t), t, at_col) for t in range(row_tiles_n)]
    n_panel = PANELS * PANEL_CHUNKS
    done = 0
    for n, (slot, left, right) in enumerate(covs):
        wendland(slot, left, right)
        if n >= 1 and done < n_panel:
            relay(done)
            done += 1
    while done < n_panel:
        relay(done)
        done += 1

    inv_copy.wait()
    for p in range(PANELS):
        inv_s[p] = split3(inv_f[p], 1)

    def own_rows(t):
        return earlier[pl.ds(t * tb, tb), :]

    def panel0(t, rows_u):
        p0 = cov[slot0(t)] - nt_dot(rows_u, got[0])
        low0[t] = nt_dot(split3(p0, 0), inv_s[0]).astype(BF)

    def panel1(t, rows_u):
        p1 = cov[slot1(t)] - nt_dot(rows_u, got[1]) - nt_dot(low0[t], low0[at_one])
        low1[t] = nt_dot(split3(p1, 0), inv_s[1]).astype(BF)

    arrived(0)
    for t in range(row_tiles_n):
        panel0(t, own_rows(t))
        if done < len(streams):
            relay(done)
            done += 1
    arrived(1)
    panel0(at_one, got[1])
    if done < len(streams):
        relay(done)
        done += 1
    for t in range(row_tiles_n):
        panel1(t, own_rows(t))
        if done < len(streams):
            relay(done)
            done += 1
    while done < len(streams):
        relay(done)
        done += 1
    arrived(PANELS)
    panel0(at_col, got[PANELS])
    panel1(at_col, got[PANELS])
    for t in range(row_tiles_n):
        out[pl.ds(t * tb, tb), :] = (
            cov[slot_out(t)]
            - nt_dot(own_rows(t), got[PANELS])
            - nt_dot(low0[t], low0[at_col])
            - nt_dot(low1[t], low1[at_col])
        )

    for s in range(len(streams)):
        for n in range(len(bits)):
            @pl.when(sends(s, n))
            def _(s=s, n=n):
                row_copy(s, n, False).wait_send()
        if streams[s][3]:
            @pl.when(dist[streams[s][0]] != 0)
            def _(s=s):
                pair_copy(s).wait_send()


def solution(mesh):
    n_row, n_col = mesh.shape["row"], mesh.shape["col"]
    n_bits = n_row.bit_length() - 1

    def local(coords, lengths, pattern, blocks, inverses, earlier):
        tb = inverses.shape[1]
        rows, width = earlier.shape
        row_tiles_n = rows // tb
        assert pattern.shape[0] == n_col and n_row == 1 << n_bits
        n_streams = PANELS * PANEL_CHUNKS + COL_CHUNKS
        n_left = row_tiles_n + 2
        smem = pl.BlockSpec(memory_space=pltpu.SMEM)
        vmem = pl.BlockSpec(memory_space=pltpu.VMEM)
        anym = pl.BlockSpec(memory_space=pl.ANY)
        sites = pl.pallas_call(
            functools.partial(pick_sites, n_row, row_tiles_n),
            out_shape=jax.ShapeDtypeStruct((n_left + 1, 8, tb), F32),
            in_specs=[smem, smem, vmem],
            out_specs=vmem,
        )(lengths, blocks, coords)
        return pl.pallas_call(
            functools.partial(kernel, n_row, n_col),
            out_shape=jax.ShapeDtypeStruct((rows, tb), F32),
            in_specs=[smem, vmem, vmem, anym],
            out_specs=vmem,
            scratch_shapes=[
                pltpu.VMEM((PANELS + 1, tb, width), BF),
                pltpu.VMEM((n_left, tb, 8), F32),
                pltpu.VMEM((n_left + 2 * row_tiles_n + 1, tb, tb), F32),
                pltpu.VMEM((PANELS, tb, tb), F32),
                pltpu.VMEM((PANELS, tb, 3 * tb), BF),
                pltpu.VMEM((n_left, tb, tb), BF),
                pltpu.VMEM((n_left, tb, tb), BF),
                pltpu.SemaphoreType.DMA((n_streams, n_bits + 1)),
                pltpu.SemaphoreType.DMA((n_streams,)),
                pltpu.SemaphoreType.DMA((n_streams,)),
                pltpu.SemaphoreType.DMA((PANELS + 1,)),
                pltpu.SemaphoreType.DMA,
            ],
            compiler_params=pltpu.CompilerParams(
                collective_id=0, has_side_effects=True, vmem_limit_bytes=56 * 1024 * 1024
            ),
        )(pattern, sites, earlier, inverses)

    return jax.shard_map(
        local,
        mesh=mesh,
        in_specs=(P(), P(), P(), P(), P(), P("row", None)),
        out_specs=P("row", "col"),
        check_vma=False,
    )
```

```python
import functools

import jax
import jax.numpy as jnp
from jax import lax
from jax.experimental import pallas as pl
from jax.experimental.pallas import tpu as pltpu
from jax.sharding import PartitionSpec as P

MESH = pl.DeviceIdType.MESH
BF = jnp.bfloat16
F32 = jnp.float32
PANELS = 2
PANEL_CHUNKS = 4
COL_CHUNKS = 4
STRIP = 32


def nt_dot(left, right):
    return lax.dot_general(left, right, (((1,), (1,)), ((), ())), preferred_element_type=F32)


def split3(x, order):
    hi = x.astype(BF)
    lo = (x - hi.astype(F32)).astype(BF)
    return jnp.concatenate([hi, hi, lo] if order == 0 else [hi, lo, hi], axis=1)


def tile_list(n_row, row_tiles_n):
    r = lax.axis_index("row")
    c = lax.axis_index("col")
    own = [jnp.int32(t * n_row) + r for t in range(row_tiles_n)]
    return own + [c, jnp.int32(1), jnp.int32(0)]


def pick_sites(n_row, row_tiles_n, lengths, blocks, coords, sites):
    tb = sites.shape[2]
    for t, tile in enumerate(tile_list(n_row, row_tiles_n)):
        start = pl.multiple_of(blocks[tile] * tb, 128)
        for comp in range(3):
            sites[t, comp : comp + 1, :] = coords[comp : comp + 1, pl.ds(start, tb)] / lengths[comp]
        sites[t, 3:8, :] = jnp.zeros((5, tb), F32)


def kernel(
    n_row,
    n_col,
    pattern,
    sites,
    earlier,
    inverses,
    out,
    got,
    sites_t,
    cov,
    inv_f,
    inv_s,
    low0,
    low1,
    send_sem,
    recv_sem,
    pair_sem,
    copy_sem,
    inv_sem,
):
    tb = inverses.shape[1]
    row_tiles_n = earlier.shape[0] // tb
    r = lax.axis_index("row")
    c = lax.axis_index("col")
    half = lax.rem(c, 2)
    mate = c + 1 - 2 * half
    bits = []
    b = n_row // 2
    while b:
        bits.append(b)
        b //= 2

    def flip(b):
        on = lax.rem(lax.div(r, b), 2)
        return r + b - 2 * b * on

    def distance(root):
        total = 0
        for b in bits:
            a1 = lax.rem(lax.div(r, b), 2)
            a2 = lax.rem(lax.div(root, b), 2)
            total = total + b * lax.rem(a1 + a2, 2)
        return total

    col_root = lax.rem(c, n_row)
    col_slot = lax.div(c, n_row)
    roots = [jnp.int32(p) for p in range(PANELS)] + [col_root]
    slots = [jnp.int32(0)] * PANELS + [col_slot]
    dist = [distance(root) for root in roots]

    half_rows = tb // 2
    p_rows = half_rows // PANEL_CHUNKS
    c_rows = tb // COL_CHUNKS
    streams = []
    for k in range(PANEL_CHUNKS):
        for p in range(PANELS):
            streams.append((p, half * half_rows + k * p_rows, p_rows, True))
    for k in range(COL_CHUNKS):
        streams.append((PANELS, jnp.int32(k * c_rows), c_rows, False))

    def piece(s, from_own):
        buf, first, rows, _ = streams[s]
        if from_own:
            start = pl.multiple_of(slots[buf] * tb + first, 16)
            return earlier.at[pl.ds(start, rows)]
        return got.at[buf, pl.ds(pl.multiple_of(first, 16), rows)]

    def row_copy(s, n, from_own):
        return pltpu.make_async_remote_copy(
            src_ref=piece(s, from_own),
            dst_ref=piece(s, False),
            send_sem=send_sem.at[s, n],
            recv_sem=recv_sem.at[s],
            device_id=(flip(bits[n]), c),
            device_id_type=MESH,
        )

    def pair_copy(s):
        return pltpu.make_async_remote_copy(
            src_ref=piece(s, False),
            dst_ref=piece(s, False),
            send_sem=send_sem.at[s, len(bits)],
            recv_sem=pair_sem.at[s],
            device_id=(r, mate),
            device_id_type=MESH,
        )

    def pair_arrival(s):
        buf, _, rows, _ = streams[s]
        k = s // PANELS
        first = pl.multiple_of((1 - half) * half_rows + k * p_rows, 16)
        there = got.at[buf, pl.ds(first, rows)]
        return pltpu.make_async_remote_copy(
            src_ref=there,
            dst_ref=there,
            send_sem=send_sem.at[s, len(bits)],
            recv_sem=pair_sem.at[s],
            device_id=(r, mate),
            device_id_type=MESH,
        )

    def sends(s, n):
        return lax.rem(dist[streams[s][0]], 2 * bits[n]) == 0

    def own_copy(buf):
        start = pl.multiple_of(slots[buf] * tb, 16)
        return pltpu.make_async_copy(
            earlier.at[pl.ds(start, tb)], got.at[buf], copy_sem.at[buf]
        )

    inv_copy = pltpu.make_async_copy(inverses, inv_f, inv_sem)
    inv_copy.start()

    barrier = pltpu.get_barrier_semaphore()
    for b in bits:
        pl.semaphore_signal(barrier, inc=1, device_id=(flip(b), c), device_id_type=MESH)
    pl.semaphore_signal(barrier, inc=1, device_id=(r, mate), device_id_type=MESH)
    pl.semaphore_wait(barrier, len(bits) + 1)

    n_panel = PANELS * PANEL_CHUNKS

    def launch(s):
        @pl.when(dist[streams[s][0]] == 0)
        def _():
            for n in range(len(bits)):
                row_copy(s, n, True).start()

    for s in range(n_panel):
        launch(s)

    for buf in range(PANELS + 1):
        @pl.when(dist[buf] == 0)
        def _(buf=buf):
            own_copy(buf).start()

    def relay(s):
        @pl.when(dist[streams[s][0]] != 0)
        def _():
            row_copy(s, 0, False).wait_recv()
            for n in range(len(bits)):
                @pl.when(sends(s, n))
                def _(n=n):
                    row_copy(s, n, False).start()
            if streams[s][3]:
                pair_copy(s).start()

    def arrived(buf):
        @pl.when(dist[buf] == 0)
        def _():
            own_copy(buf).wait()

        for s in range(len(streams)):
            if streams[s][0] == buf and streams[s][3]:
                @pl.when(dist[buf] != 0)
                def _(s=s):
                    pair_arrival(s).wait_recv()

    tiles = tile_list(n_row, row_tiles_n)
    n_left = row_tiles_n + 2
    at_col, at_one, at_zero = row_tiles_n, row_tiles_n + 1, row_tiles_n + 2
    for t in range(n_left):
        sites_t[t] = sites[t].T

    def wendland(slot, left, right):
        keep = pattern[tiles[left], tiles[right]].astype(F32)

        def strip(i, carry):
            rows = pl.ds(pl.multiple_of(i * STRIP, STRIP), STRIP)
            at = sites_t[left, rows, :]
            sq = None
            for comp in range(3):
                off = at[:, comp : comp + 1] - sites[right, comp : comp + 1, :]
                sq = off * off if sq is None else sq + off * off
            radius = jnp.sqrt(sq)
            fall = jnp.maximum(1.0 - radius, 0.0)
            fall = fall * fall
            cov[slot, rows, :] = fall * fall * (4.0 * radius + 1.0) * keep
            return carry

        lax.fori_loop(0, tb // STRIP, strip, 0)

    def slot0(t):
        return t

    def slot1(t):
        return n_left + t

    def slot_out(t):
        return n_left + row_tiles_n + 1 + t

    covs = [(slot0(t), t, at_zero) for t in range(n_left)]
    covs += [(slot1(t), t, at_one) for t in range(row_tiles_n + 1)]
    covs += [(slot_out(t), t, at_col) for t in range(row_tiles_n)]
    done = 0
    sent = n_panel
    for n, (slot, left, right) in enumerate(covs):
        wendland(slot, left, right)
        if n == 1:
            inv_copy.wait()
            for p in range(PANELS):
                inv_s[p] = split3(inv_f[p], 1)
        if n >= 1 and done < n_panel:
            relay(done)
            done += 1
            if done >= n_panel // 2 and sent < len(streams):
                launch(sent)
                sent += 1
    while done < n_panel:
        relay(done)
        done += 1
    while sent < len(streams):
        launch(sent)
        sent += 1

    def own_rows(t):
        return earlier[pl.ds(t * tb, tb), :]

    def panel0(t, rows_u):
        p0 = cov[slot0(t)] - nt_dot(rows_u, got[0])
        low0[t] = nt_dot(split3(p0, 0), inv_s[0]).astype(BF)

    def panel1(t, rows_u):
        p1 = cov[slot1(t)] - nt_dot(rows_u, got[1]) - nt_dot(low0[t], low0[at_one])
        low1[t] = nt_dot(split3(p1, 0), inv_s[1]).astype(BF)

    arrived(0)
    for t in range(row_tiles_n):
        panel0(t, own_rows(t))
        if t >= 1 and done < len(streams):
            relay(done)
            done += 1
    arrived(1)
    panel0(at_one, got[1])
    if done < len(streams):
        relay(done)
        done += 1
    for t in range(row_tiles_n):
        panel1(t, own_rows(t))
        if done < len(streams):
            relay(done)
            done += 1
    while done < len(streams):
        relay(done)
        done += 1
    arrived(PANELS)
    panel0(at_col, got[PANELS])
    panel1(at_col, got[PANELS])
    for t in range(row_tiles_n):
        out[pl.ds(t * tb, tb), :] = (
            cov[slot_out(t)]
            - nt_dot(own_rows(t), got[PANELS])
            - nt_dot(low0[t], low0[at_col])
            - nt_dot(low1[t], low1[at_col])
        )

    for s in range(len(streams)):
        for n in range(len(bits)):
            @pl.when(sends(s, n))
            def _(s=s, n=n):
                row_copy(s, n, False).wait_send()
        if streams[s][3]:
            @pl.when(dist[streams[s][0]] != 0)
            def _(s=s):
                pair_copy(s).wait_send()


def solution(mesh):
    n_row, n_col = mesh.shape["row"], mesh.shape["col"]
    n_bits = n_row.bit_length() - 1

    def local(coords, lengths, pattern, blocks, inverses, earlier):
        tb = inverses.shape[1]
        rows, width = earlier.shape
        row_tiles_n = rows // tb
        assert pattern.shape[0] == n_col and n_row == 1 << n_bits
        n_streams = PANELS * PANEL_CHUNKS + COL_CHUNKS
        n_left = row_tiles_n + 2
        smem = pl.BlockSpec(memory_space=pltpu.SMEM)
        vmem = pl.BlockSpec(memory_space=pltpu.VMEM)
        anym = pl.BlockSpec(memory_space=pl.ANY)
        sites = pl.pallas_call(
            functools.partial(pick_sites, n_row, row_tiles_n),
            out_shape=jax.ShapeDtypeStruct((n_left + 1, 8, tb), F32),
            in_specs=[smem, smem, vmem],
            out_specs=vmem,
        )(lengths, blocks, coords)
        return pl.pallas_call(
            functools.partial(kernel, n_row, n_col),
            out_shape=jax.ShapeDtypeStruct((rows, tb), F32),
            in_specs=[smem, vmem, vmem, anym],
            out_specs=vmem,
            scratch_shapes=[
                pltpu.VMEM((PANELS + 1, tb, width), BF),
                pltpu.VMEM((n_left, tb, 8), F32),
                pltpu.VMEM((n_left + 2 * row_tiles_n + 1, tb, tb), F32),
                pltpu.VMEM((PANELS, tb, tb), F32),
                pltpu.VMEM((PANELS, tb, 3 * tb), BF),
                pltpu.VMEM((n_left, tb, tb), BF),
                pltpu.VMEM((n_left, tb, tb), BF),
                pltpu.SemaphoreType.DMA((n_streams, n_bits + 1)),
                pltpu.SemaphoreType.DMA((n_streams,)),
                pltpu.SemaphoreType.DMA((n_streams,)),
                pltpu.SemaphoreType.DMA((PANELS + 1,)),
                pltpu.SemaphoreType.DMA,
            ],
            compiler_params=pltpu.CompilerParams(
                collective_id=0, has_side_effects=True, vmem_limit_bytes=56 * 1024 * 1024
            ),
        )(pattern, sites, earlier, inverses)

    return jax.shard_map(
        local,
        mesh=mesh,
        in_specs=(P(), P(), P(), P(), P(), P("row", None)),
        out_specs=P("row", "col"),
        check_vma=False,
    )
```
